128 devices in a mesh: tile: 32 (over x, y_lo, z), mem: 4 (over y_hi, core).
Axes of the slice: x: 4, y: 4 (y_hi: 2, y_lo: 2; y = y_hi * 2 + y_lo), z: 4, core: 2. Of those that a mesh axis runs over, the one named last changes fastest.
Arguments:
- alpha: float32 [4, 16, 64, 4096], P('mem', None, None, 'tile'), may hold values from -6 to 6
- members: bfloat16 [4, 16, 64, 4096], P('mem', None, None, 'tile'), may hold values from -6 to 6
- mem_weight: float32 [4], P('mem'), may hold values from 0.5 to 2
- kappa: float32 [64, 4096], P(None, 'tile'), may hold values from 0.04 to 0.24
- norm_scale: float32 [64, 4096], P(None, 'tile'), may hold values from 0.8 to 1.25
- land_sea: int32 [64, 4096], P(None, 'tile'), may hold values 0 or 1
- obs_cell: int32 [65536], P('tile'), may hold values from 0 to 131071
- obs_weight: float32 [65536], P('tile'), may hold values from 0.5 to 4
Outputs:
- product: float32 [4, 16, 64, 4096], P('mem', None, None, 'tile')
The draws below stay inside these ranges and needn't reach their ends.
Inputs may be any that keep to these rules, and one draw needn't show every extreme that they name: `obs_cell`: observations o of tile t = o // 2048 index a cell of that tile; several may share a cell.
All inputs are finite; a program needn't handle non-finite values. No bound on the sum of `land_sea` on one device may be relied on, other than what follows from the above.
Results may differ from the reference program's by a relative error of at most 0.0003.
Values sent between devices are 32-bit elements; how exact they have to be, the bound alone decides.
A program may use at most 64 MiB of HBM per device.

```python
import math
import jax
import jax.numpy as jnp
from jax import lax

LEV = 16
NY = 64
NXT = 128
STEPS = 8
OBS_DEV = 2048
MEM = 4
NX = 4096
N_TILE = 32


def with_ends(drawn, rng, least, high):
    place = [jax.random.randint(jax.random.fold_in(rng, axis), (), 0, length) for axis, length in enumerate(drawn.shape)]
    main_axis = drawn.shape.index(max(drawn.shape))
    next_to = place[:main_axis] + [(place[main_axis] + 1) % drawn.shape[main_axis]] + place[main_axis + 1:]
    return drawn.at[tuple(place)].set(least).at[tuple(next_to)].set(high)


def block_levels(own_key, shape, shards, low, largest):
    factor_of, own = 1.0, jax.random.fold_in(own_key, 6)
    for dim, blocks in shards:
        draws = jnp.exp(jax.random.uniform(jax.random.fold_in(own, dim), (blocks,), jnp.float32, low / len(shards), largest / len(shards)))
        factor_of = factor_of * jnp.repeat(draws, shape[dim] // blocks).reshape([-1 if axis == dim else 1 for axis in range(len(shape))])
    return factor_of


def bell_draw(rng, shape, deviation, bound, pieces=(), held_as=jnp.bfloat16):
    level = block_levels(rng, shape, pieces, -0.22, 0.18) if pieces else 1.0
    values = jax.random.normal(rng, shape, jnp.float32) * deviation * level
    return jnp.minimum(jnp.maximum(values, -bound), bound).astype(held_as)


def setup_inputs(seed: int = 0) -> dict:
    splits = jax.random.split(jax.random.key(seed), 9)
    return {
        "alpha": bell_draw(splits[0], (MEM, LEV, NY, NX), 1.0, 6.0, ((0, 4), (3, 32)), jnp.float32),
        "members": bell_draw(splits[1], (MEM, LEV, NY, NX), 1.0, 6.0, ((0, 4), (3, 32))),
        "mem_weight": jnp.clip(jnp.exp(math.log(2.0) - 1.3862944 * jax.random.uniform(splits[2], (MEM,), jnp.float32) ** block_levels(splits[2], (MEM,), ((0, 4),), -0.2, 0.2)), 0.5, 2.0),
        "kappa": jnp.clip(0.04 + 0.19999999552965164 * jax.random.uniform(splits[3], (NY, NX), jnp.float32) ** block_levels(splits[3], (NY, NX), ((1, 32),), -0.2, 0.2), 0.04, 0.24),
        "norm_scale": jnp.clip(0.8 + 0.45 * jax.random.uniform(splits[4], (NY, NX), jnp.float32) ** block_levels(splits[4], (NY, NX), ((1, 32),), -0.2, 0.2), 0.8, 1.25),
        "land_sea": with_ends((jax.random.randint(splits[5], (NY, NX), 0, 5) < 4).astype(jnp.int32), jax.random.fold_in(splits[5], 1), 0, 1),
        "obs_cell": with_ends(jax.random.randint(splits[6], (N_TILE * OBS_DEV,), 0, LEV * NY * NXT), jax.random.fold_in(splits[6], 1), 0, (LEV * NY * NXT) - 1).astype(jnp.int32),
        "obs_weight": jnp.clip(jnp.exp(math.log(4.0) - 2.0794415 * jax.random.uniform(splits[7], (N_TILE * OBS_DEV,), jnp.float32) ** block_levels(splits[7], (N_TILE * OBS_DEV,), ((0, 32),), -0.2, 0.2)), 0.5, 4.0),
    }


def shift_up(u):
    return jnp.concatenate([u[..., 1:, :], jnp.zeros_like(u[..., :1, :])], -2)


def shift_down(u):
    return jnp.concatenate([jnp.zeros_like(u[..., :1, :]), u[..., :-1, :]], -2)


def faces(kappa, land_sea):
    ocean = land_sea.astype(jnp.float32)
    east = 0.5 * (kappa + jnp.roll(kappa, -1, 1)) * ocean * jnp.roll(ocean, -1, 1)
    north = 0.5 * (kappa[:-1] + kappa[1:]) * ocean[:-1] * ocean[1:]
    north = jnp.concatenate([north, jnp.zeros((1, north.shape[1]), jnp.float32)], 0)
    return east, north


def smooth(u, east, north):
    across = east * (jnp.roll(u, -1, -1) - u) - jnp.roll(east, 1, 1) * (u - jnp.roll(u, 1, -1))
    along = north * (shift_up(u) - u) - shift_down(north) * (u - shift_down(u))
    return u + across + along


def reference(alpha, members, mem_weight, kappa, norm_scale, land_sea, obs_cell, obs_weight):
    east, north = faces(kappa, land_sea)

    def forward(u):
        for step in range(STEPS):
            u = smooth(norm_scale * u, east, north)
        return u

    def adjoint(u):
        for step in range(STEPS):
            u = norm_scale * smooth(u, east, north)
        return u

    def accumulate(total, item):
        field, member, weight = item
        return total + weight * member.astype(jnp.float32) * forward(field), None

    start = jnp.zeros((LEV, NY, NX), jnp.float32)
    increment, unused = lax.scan(accumulate, start, (alpha, members, mem_weight))
    owner = (jnp.arange(N_TILE * OBS_DEV, dtype=jnp.int32) // OBS_DEV).astype(jnp.int32)
    level = obs_cell // (NY * NXT)
    row = (obs_cell // NXT) % NY
    column = obs_cell % NXT + owner * NXT
    flat = ((level * NY + row) * NX + column).astype(jnp.int32)
    obs_field = jnp.zeros((LEV * NY * NX,), jnp.float32).at[flat].add(obs_weight).reshape(LEV, NY, NX)
    gradient = obs_field * increment

    def finish(item):
        field, member, weight = item
        return field + adjoint(weight * member.astype(jnp.float32) * gradient)

    return lax.map(finish, (alpha, members, mem_weight))
```

```python
import functools

import jax
import jax.numpy as jnp
from jax import lax
from jax.experimental import pallas as pl
from jax.experimental.pallas import tpu as pltpu
from jax.sharding import PartitionSpec as P

STEPS = 8
LANES = 128
HALO = 8
HALF = 64
EXT = HALF + HALO
BF = jnp.bfloat16
F32 = jnp.float32
MESH = pl.DeviceIdType.MESH
C0, C1, I0, I1, A01, N1, S0 = range(7)


def low_half(shape):
    return lax.broadcasted_iota(jnp.int32, shape, len(shape) - 1) < HALF


def exchange_halves(a, b):
    low = low_half(a.shape)
    swapped = pltpu.roll(jnp.where(low, b, a), HALF, a.ndim - 1)
    return jnp.where(low, a, swapped), jnp.where(low, swapped, b)


def kernel(
    alpha, members, mem_weight, kappa, norm, land, cell, weight, out,
    a_v, m_v, k_v, n_v, l_v, cell_v, w_v, o_v, mf_v, wide, fields, packed, cf,
    mem_u, buf_a, buf_b, halo_l, halo_r, back_l, back_r, edge_l, edge_r,
    field_send_l, field_send_r, field_l, field_r, onehot, pt_v, q_v, val_v, peers,
    in_sem, out_sem, send_sem, recv_sem,
):
    tiles, mems = lax.axis_size("tile"), lax.axis_size("mem")
    me_t, me_m = lax.axis_index("tile"), lax.axis_index("mem")
    right, left = lax.rem(me_t + 1, tiles), lax.rem(me_t + tiles - 1, tiles)

    barrier = pltpu.get_barrier_semaphore()
    for neighbour in (left, right):
        pl.semaphore_signal(barrier, inc=1, device_id={"tile": neighbour}, device_id_type=MESH)
    for k in range(1, mems):
        pl.semaphore_signal(barrier, inc=1, device_id={"mem": lax.rem(me_m + k, mems)}, device_id_type=MESH)

    loads = [
        pltpu.make_async_copy(src, dst, in_sem.at[i])
        for i, (src, dst) in enumerate(
            ((kappa, k_v), (norm, n_v), (land, l_v), (cell, cell_v), (weight, w_v), (alpha, a_v), (members, m_v))
        )
    ]
    for copy in loads:
        copy.start()

    def send(i, src, dst, **device):
        copy = pltpu.make_async_remote_copy(
            src_ref=src, dst_ref=dst, send_sem=send_sem.at[i], recv_sem=recv_sem.at[i],
            device_id=device, device_id_type=MESH,
        )
        copy.start()
        return copy

    wide2 = wide.reshape(LANES * 8, LANES)
    fields2 = fields.reshape((LANES + 2 * HALO) * 8, LANES)
    cf2 = cf.reshape(EXT * 8, LANES)

    for copy in loads[:3]:
        copy.wait()

    def field_rows(f, r):
        ref = (k_v, n_v, l_v)[f]
        return ref[pl.ds(r, 32, stride=2), :].astype(F32)

    for f in range(3):
        even, odd = field_rows(f, 0), field_rows(f, 1)
        turned = jnp.concatenate([even, even, odd, odd], 0).T
        fields2[pl.ds(HALO * 8 + f, LANES, stride=8), :] = turned
        field_send_l[f] = turned[:HALO]
        field_send_r[f] = turned[LANES - HALO:]

    q_rows = [jnp.sqrt(field_rows(1, r)) for r in range(2)]
    loads[5].wait()

    def turn_in(load, dst2):
        for l in range(8):
            rows = [load(l, 0), load(l + 8, 0), load(l, 1), load(l + 8, 1)]
            dst2[pl.ds(l, LANES, stride=8), :] = jnp.concatenate(rows, 0).T

    turn_in(lambda lev, r: a_v[pl.ds(64 * lev + r, 32, stride=2), :] * q_rows[r], wide2)

    pl.semaphore_wait(barrier, mems + 1)
    halo_copies = [
        send(0, field_send_l, field_r, tile=left),
        send(1, field_send_r, field_l, tile=right),
        send(2, wide.at[pl.ds(0, HALO)], halo_r, tile=left),
        send(3, wide.at[pl.ds(LANES - HALO, HALO)], halo_l, tile=right),
    ]

    def pack(load_a, load_b, first, count, store):
        for c in range(first, first + count, 8):
            a = jnp.stack([load_a(c + k) for k in range(8)])
            b = jnp.stack([load_b(c + k) for k in range(8)])
            u0, u1 = exchange_halves(a, b)
            store(c, u0, u1)

    def into(dst, first):
        def store(c, u0, u1):
            dst[0, pl.ds(first + c, 8)] = u0
            dst[1, pl.ds(first + c, 8)] = u1
        return store

    def pack_center(src, dst, first):
        pack(lambda c: src[c], lambda c: src[LANES - 1 - c], 0, HALF, into(dst, first))

    def pack_halo(from_left, from_right, dst):
        pack(lambda c: from_left[c], lambda c: from_right[HALO - 1 - c], 0, HALO, into(dst, 0))

    pack_center(wide, buf_a, HALO)

    def pack_fields(first, count):
        last = LANES + 2 * HALO - 1
        pack(lambda c: fields[c], lambda c: fields[last - c], first, count, into(packed, 0))

    def coefficients(first, count):
        def get(r, f, shift=0):
            return packed2[pl.ds((r * (EXT + 1) + first + shift) * 8 + f, count, stride=8), :]
        packed2 = packed.reshape(2 * (EXT + 1) * 8, LANES)
        row = lax.broadcasted_iota(jnp.int32, (count, LANES), 1) & 31
        back, ahead = (lambda x: pltpu.roll(x, 1, 1)), (lambda x: pltpu.roll(x, LANES - 1, 1))
        k0, k1, d0, d1, o0, o1 = get(0, 0), get(1, 0), get(0, 1), get(1, 1), get(0, 2), get(1, 2)
        def face(ka, kb, oa, ob):
            return 0.5 * (ka + kb) * oa * ob
        inner0 = face(k0, get(0, 0, 1), o0, get(0, 2, 1))
        inner1 = face(k1, get(1, 0, 1), o1, get(1, 2, 1))
        between = face(k0, k1, o0, o1)
        above = jnp.where(row == 31, 0.0, face(k1, ahead(k0), o1, ahead(o0)))
        below = back(above)
        if first == 0:
            prior0 = prior1 = None
            zero = jnp.zeros((1, LANES), F32)
            prior0 = jnp.concatenate([zero, inner0[:-1]], 0)
            prior1 = jnp.concatenate([zero, inner1[:-1]], 0)
        else:
            prior0 = face(k0, get(0, 0, -1), o0, get(0, 2, -1))
            prior1 = face(k1, get(1, 0, -1), o1, get(1, 2, -1))
        q0, q1 = jnp.sqrt(d0), jnp.sqrt(d1)
        def put(k, value):
            cf2[pl.ds(first * 8 + k, count, stride=8), :] = value
        put(C0, d0 * (1.0 - inner0 - prior0 - between - below))
        put(C1, d1 * (1.0 - inner1 - prior1 - between - above))
        put(I0, inner0 * q0 * jnp.sqrt(get(0, 1, 1)))
        put(I1, inner1 * q1 * jnp.sqrt(get(1, 1, 1)))
        put(A01, between * q0 * q1)
        put(N1, above * q1 * ahead(q0))
        put(S0, below * q0 * back(q1))

    pack_fields(HALO, HALF)
    for r in range(2):
        packed[r, EXT] = pltpu.roll(packed[r, EXT - 1], HALF, 1)
    coefficients(HALO, HALF)

    def coef(k, c, n):
        return jnp.broadcast_to(cf[pl.ds(c, n), k:k + 1, :], (n, 8, LANES))

    def step(src, dst, lo, hi):
        for c in range(lo, hi, 8):
            n = min(8, hi - c)
            if c + n == EXT:
                x0, x1 = src[0, pl.ds(c - 1, n + 1)], src[1, pl.ds(c - 1, n + 1)]
                x0 = jnp.concatenate([x0, pltpu.roll(x0[n:], HALF, 2)], 0)
                x1 = jnp.concatenate([x1, pltpu.roll(x1[n:], HALF, 2)], 0)
            else:
                x0, x1 = src[0, pl.ds(c - 1, n + 2)], src[1, pl.ds(c - 1, n + 2)]
            i0, i1, both = coef(I0, c - 1, n + 1), coef(I1, c - 1, n + 1), coef(A01, c, n)
            m0, m1 = x0[1:n + 1], x1[1:n + 1]
            dst[0, pl.ds(c, n)] = (
                (coef(C0, c, n) * m0 + i0[1:] * x0[2:]) + (i0[:n] * x0[:n] + both * m1)
            ) + coef(S0, c, n) * pltpu.roll(m1, 1, 2)
            dst[1, pl.ds(c, n)] = (
                (coef(C1, c, n) * m1 + i1[1:] * x1[2:]) + (i1[:n] * x1[:n] + both * m0)
            ) + coef(N1, c, n) * pltpu.roll(m0, LANES - 1, 2)

    bufs = (buf_a, buf_b)

    def center():
        for t in range(1, STEPS + 1):
            step(bufs[(t - 1) % 2], bufs[t % 2], HALO + t, EXT)

    def wedge():
        for t in range(1, STEPS + 1):
            step(bufs[(t - 1) % 2], bufs[t % 2], t, HALO + t)

    center()

    loads[3].wait()
    cells = cell_v[...]
    level, row, column = cells >> 13, (cells >> 7) & 63, cells & 127
    second = column >> 6
    place = jnp.where(second == 1, LANES - 1 - column, column)
    obs_row = (((row & 1) * HALF + place) * 8 + (level & 7)).astype(jnp.int16)
    obs_lane = second * HALF + (level >> 3) * 32 + (row >> 1)
    index = lax.broadcasted_iota(jnp.int16, (LANES, LANES), 0)
    for j in range(16):
        mine = obs_row[j:j + 1]
        def fill(i, carry, mine=mine, j=j):
            hit = (index + (i * LANES).astype(jnp.int16)) == mine
            onehot[pl.ds(pl.multiple_of(i * LANES, LANES), LANES), pl.ds(j * LANES, LANES)] = jnp.where(
                hit, jnp.ones((), BF), jnp.zeros((), BF)
            )
            return carry
        lax.fori_loop(0, 8, fill, 0)

    loads[6].wait()
    own_weight = mem_weight[0] / jnp.sqrt(n_v[...])
    for lev in range(16):
        mf_v[pl.ds(64 * lev, 64), :] = m_v[pl.ds(64 * lev, 64), :].astype(F32) * own_weight

    for copy in halo_copies:
        copy.wait()
    for f in range(3):
        fields2[pl.ds(f, HALO, stride=8), :] = field_l[f]
        fields2[pl.ds((LANES + HALO) * 8 + f, HALO, stride=8), :] = field_r[f]
    pack_fields(0, HALO)
    coefficients(0, 2 * HALO)
    pack_halo(halo_l, halo_r, buf_a)
    turn_in(lambda lev, r: mf_v[pl.ds(64 * lev + r, 32, stride=2), :], wide2)
    pack_center(wide, mem_u, 0)
    wedge()

    for i in range(8):
        r, c = i // 4, (i % 4) * 16
        term = (buf_a[r, pl.ds(HALO + c, 16)] * mem_u[r, pl.ds(c, 16)]).reshape(LANES, LANES).T
        high = term.astype(BF)
        pt_v[0:LANES, i * LANES:(i + 1) * LANES] = high
        pt_v[LANES:, i * LANES:(i + 1) * LANES] = (term - high.astype(F32)).astype(BF)
    lane = lax.broadcasted_iota(jnp.int32, (LANES, LANES), 0)
    for j in range(0, 16, 2):
        g = jnp.dot(pt_v[...], onehot[:, j * LANES:(j + 2) * LANES], preferred_element_type=F32)
        for k in range(2):
            both = g[:LANES, k * LANES:(k + 1) * LANES] + g[LANES:, k * LANES:(k + 1) * LANES]
            hit = lane == obs_lane[j + k:j + k + 1]
            val_v[j + k:j + k + 1, :] = jnp.sum(jnp.where(hit, both, 0.0), axis=0, keepdims=True)

    sums = [
        send(4 + k, val_v, peers.at[k - 1], mem=lax.rem(me_m + k, mems)) for k in range(1, mems)
    ]
    for copy in sums:
        copy.wait()
    loads[4].wait()
    total = val_v[...]
    for k in range(mems - 1):
        total = total + peers[k]
    total = total * w_v[...]
    high = total.astype(BF).astype(F32)
    rest = total - high
    for j in range(16):
        hit = lane == obs_lane[j:j + 1]
        q_v[0:LANES, j * LANES:(j + 1) * LANES] = jnp.where(hit, high[j:j + 1], 0.0).astype(BF)
        q_v[LANES:, j * LANES:(j + 1) * LANES] = jnp.where(hit, rest[j:j + 1], 0.0).astype(BF)
    for i in range(4):
        g = lax.dot_general(
            onehot[pl.ds(i * 256, 256), :], q_v[...], (((1,), (1,)), ((), ())), preferred_element_type=F32
        )
        r, c = i // 2, (i % 2) * 32
        gradient = (g[:, :LANES] + g[:, LANES:]).reshape(32, 8, LANES)
        buf_a[r, pl.ds(HALO + c, 32)] = gradient * mem_u[r, pl.ds(c, 32)]

    edge_a, edge_b = exchange_halves(buf_a[0, pl.ds(HALO, 8)], buf_a[1, pl.ds(HALO, 8)])
    edge_l[...] = edge_a
    for k in range(HALO):
        edge_r[HALO - 1 - k] = edge_b[k]
    back_copies = [send(8, edge_l, back_r, tile=left), send(9, edge_r, back_l, tile=right)]
    center()
    for copy in back_copies:
        copy.wait()
    pack_halo(back_l, back_r, buf_a)
    wedge()

    for c in range(0, HALF, 8):
        a, b = exchange_halves(buf_a[0, pl.ds(HALO + c, 8)], buf_a[1, pl.ds(HALO + c, 8)])
        wide[pl.ds(c, 8)] = a
        for k in range(8):
            wide[LANES - 1 - c - k] = b[k]
    stores = []
    for l in range(8):
        rows = wide2[pl.ds(l, LANES, stride=8), :].T
        for k, (lev, r) in enumerate(((l, 0), (l + 8, 0), (l, 1), (l + 8, 1))):
            where = pl.ds(64 * lev + r, 32, stride=2)
            o_v[where, :] = a_v[where, :] + rows[32 * k:32 * k + 32] * q_rows[r]
        for k, lev in enumerate((l, l + 8)):
            part = pl.ds(64 * lev, 64)
            copy = pltpu.make_async_copy(o_v.at[part], out.at[part], out_sem.at[lev])
            copy.start()
            stores.append(copy)
    for copy in stores:
        copy.wait()


def local(alpha, members, mem_weight, kappa, norm_scale, land_sea, obs_cell, obs_weight):
    shape = alpha.shape
    rows = 16 * 64
    vm = pltpu.VMEM
    sq = (8, LANES)
    any_spec = pl.BlockSpec(memory_space=pl.ANY)
    result = pl.pallas_call(
        kernel,
        out_shape=jax.ShapeDtypeStruct((rows, LANES), F32),
        in_specs=[any_spec, any_spec, pl.BlockSpec(memory_space=pltpu.SMEM)] + [any_spec] * 5,
        out_specs=any_spec,
        scratch_shapes=[
            vm((rows, LANES), F32), vm((rows, LANES), BF), vm((64, LANES), F32), vm((64, LANES), F32),
            vm((64, LANES), jnp.int32), vm((16, LANES), jnp.int32), vm((16, LANES), F32),
            vm((rows, LANES), F32), vm((rows, LANES), F32),
            vm((LANES, *sq), F32), vm((LANES + 2 * HALO, *sq), F32), vm((2, EXT + 1, *sq), F32), vm((EXT, *sq), F32),
            vm((2, HALF, *sq), F32), vm((2, EXT, *sq), F32), vm((2, EXT, *sq), F32),
            *[vm((HALO, *sq), F32) for _ in range(6)],
            *[vm((3, HALO, LANES), F32) for _ in range(4)],
            vm((rows, 2048), BF), vm((256, rows), BF), vm((256, 2048), BF),
            vm((16, LANES), F32), vm((3, 16, LANES), F32),
            pltpu.SemaphoreType.DMA((7,)), pltpu.SemaphoreType.DMA((16,)),
            pltpu.SemaphoreType.DMA((10,)), pltpu.SemaphoreType.DMA((10,)),
        ],
        compiler_params=pltpu.CompilerParams(
            collective_id=0, has_side_effects=True, vmem_limit_bytes=40 * 2**20
        ),
    )(
        alpha.reshape(rows, LANES), members.reshape(rows, LANES), mem_weight, kappa, norm_scale, land_sea,
        obs_cell.reshape(16, LANES), obs_weight.reshape(16, LANES),
    )
    return result.reshape(shape)


def solution(mesh):
    placed = (
        P("mem", None, None, "tile"),
        P("mem", None, None, "tile"),
        P("mem"),
        P(None, "tile"),
        P(None, "tile"),
        P(None, "tile"),
        P("tile"),
        P("tile"),
    )
    return jax.shard_map(
        local, mesh=mesh, in_specs=placed, out_specs=P("mem", None, None, "tile"), check_vma=False
    )
```
